32 devices in a mesh: dp: 4 (over y, x), seq: 8 (over z, core).
Axes of the slice: x: 2, y: 2, z: 4, core: 2. Of those that a mesh axis runs over, the one named last changes fastest.
Arguments:
- query: bfloat16 [4, 6144, 1536], P('dp', 'seq'), may hold values from -6 to 6
- key_states: bfloat16 [4, 6144, 1536], P('dp', 'seq'), may hold values from -6 to 6
- value_states: bfloat16 [4, 6144, 1536], P('dp', 'seq'), may hold values from -6 to 6
- attn_out: bfloat16 [4, 6144, 1536], P('dp', 'seq'), may hold values from -0.59765625 to 0.59765625
- log_norm: float32 [4, 12, 6144], P('dp', None, 'seq'), may hold values from 6 to 7
- out_grad: bfloat16 [4, 6144, 3072], P('dp', 'seq'), may hold values from -24 to 24
- out_weight: bfloat16 [1536, 3072], P('dp'), may hold values from -0.15625 to 0.15625
- tile_lists: int32 [4, 16, 3], P('dp'), may hold values from 0 to 15, as said below
Outputs:
- query_grad: bfloat16 [4, 6144, 1536], P('dp', 'seq')
- key_grad: bfloat16 [4, 6144, 1536], P('dp', 'seq')
- value_grad: bfloat16 [4, 6144, 1536], P('dp', 'seq')
- weight_grad: float32 [1536, 3072], P('dp')
The draws below stay inside these ranges and needn't reach their ends.
Inputs may be any that keep to these rules, and one draw needn't show every extreme that they name: `tile_lists`: row i of a clip's list names 3 different tiles: tile i itself and tiles j with (i // 2) * 2 - 1 <= j <= (i // 2) * 2 + 2.
All inputs are finite; a program needn't handle non-finite values.
Results may differ from the reference program's by a relative error of at most 0.0095.
Values may be sent and summed in bfloat16 or wider, within the bound.
A program may use at most 256 MiB of HBM per device.

```python
import math
import jax
import jax.numpy as jnp
from jax import lax

D = 3072
HEADS = 12
HD = 128
TILE = 384
KEEP = 3
TPD = 2
TOK_DEV = 768
CLIP_TOK = 6144
CLIP_TILES = 16
CLIPS = 4
HH = 1536
N_SEQ = 8


def draw_tile_lists(key, part):
    span = TPD + 2
    tile_index = jnp.arange(CLIP_TILES, dtype=jnp.int32)
    tile_slab = tile_index // TPD
    candidate = jnp.arange(span, dtype=jnp.int32)
    candidate_tile = tile_slab[:, None] * TPD - 1 + candidate[None, :]
    in_range = (candidate_tile >= 0) & (candidate_tile < CLIP_TILES)
    is_self = candidate_tile == tile_index[:, None]
    random_bits = jax.random.randint(key, (CLIPS, CLIP_TILES, span), 0, 1 << 20, dtype=jnp.int32)
    priority = random_bits * 64 + candidate[None, None, :]
    priority = jnp.where(is_self[None], jnp.int32(1 << 27), jnp.where(in_range[None], priority, jnp.int32(-1)))
    chosen = lax.top_k(priority, KEEP)[1]
    full_tiles = jnp.broadcast_to(candidate_tile[None], (CLIPS, CLIP_TILES, span))
    return jnp.take_along_axis(full_tiles, chosen, axis=2).astype(jnp.int32)


def steps_of(stream_key, dims, shards, low, top_value):
    def one(axis_at, parts):
        heights = jax.random.uniform(jax.random.fold_in(jax.random.fold_in(stream_key, 6), axis_at), (parts,), jnp.float32, low / len(shards), top_value / len(shards))
        return jnp.repeat(jnp.exp(heights), dims[axis_at] // parts).reshape((-1,) + (1,) * (len(dims) - axis_at - 1))

    level = one(*shards[0])
    for cut in shards[1:]:
        level = level * one(*cut)
    return level


def bell_draw(stream_key, extent, scale, most, cuts=(), kind=jnp.bfloat16):
    array = scale * jax.random.normal(stream_key, extent, jnp.float32)
    if cuts:
        array = array * steps_of(stream_key, extent, cuts, -0.22, 0.18)
    return jnp.clip(array, -most, most).astype(kind)


def setup_inputs(seed: int = 0) -> dict:
    streams_of = jax.random.split(jax.random.key(seed), 9)
    return {
        "query": bell_draw(streams_of[0], (CLIPS, CLIP_TOK, HH), 1.0, 6.0, ((0, 4), (1, 8))),
        "key_states": bell_draw(streams_of[1], (CLIPS, CLIP_TOK, HH), 1.0, 6.0, ((0, 4), (1, 8))),
        "value_states": bell_draw(streams_of[2], (CLIPS, CLIP_TOK, HH), 1.0, 6.0, ((0, 4), (1, 8))),
        "attn_out": bell_draw(streams_of[3], (CLIPS, CLIP_TOK, HH), 0.1, 0.59765625, ((0, 4), (1, 8))),
        "log_norm": jnp.clip(6.0 + 1.0 * jax.random.uniform(streams_of[4], (CLIPS, HEADS, CLIP_TOK), jnp.float32) ** steps_of(streams_of[4], (CLIPS, HEADS, CLIP_TOK), ((0, 4), (2, 8)), -0.2, 0.2), 6.0, 7.0),
        "out_grad": bell_draw(streams_of[5], (CLIPS, CLIP_TOK, D), 4.0, 24.0, ((0, 4), (1, 8))),
        "out_weight": bell_draw(streams_of[6], (HH, D), HH ** -0.5, 0.15625, ((0, 4),)),
        "tile_lists": draw_tile_lists(jax.random.fold_in(streams_of[8], 71), 0),
    }


def slab_terms(query, key_pad, value_pad, attn_grad, log_norm, row_delta, tile_lists, slab_index):
    score_scale = 1.0 / math.sqrt(HD)
    window_rows = TOK_DEV + 2 * TILE
    row_start = (slab_index * TOK_DEV).astype(jnp.int32)
    q_rows = lax.dynamic_slice_in_dim(query, row_start, TOK_DEV, 0).astype(jnp.float32).reshape(TOK_DEV, HEADS, HD)
    g_rows = lax.dynamic_slice_in_dim(attn_grad, row_start, TOK_DEV, 0).astype(jnp.float32).reshape(TOK_DEV, HEADS, HD)
    norm_rows = lax.dynamic_slice_in_dim(log_norm, row_start, TOK_DEV, 1)
    delta_rows = lax.dynamic_slice_in_dim(row_delta, row_start, TOK_DEV, 1)
    key_window = lax.dynamic_slice_in_dim(key_pad, row_start, window_rows, 0).astype(jnp.float32).reshape(window_rows, HEADS, HD)
    value_window = lax.dynamic_slice_in_dim(value_pad, row_start, window_rows, 0).astype(jnp.float32).reshape(window_rows, HEADS, HD)
    slab_lists = lax.dynamic_slice_in_dim(tile_lists, (slab_index * TPD).astype(jnp.int32), TPD, 0)
    window_ids = (slab_index * TPD - 1).astype(jnp.int32) + jnp.arange(TPD + 2, dtype=jnp.int32)
    tile_mask = jnp.any(slab_lists[:, :, None] == window_ids[None, None, :], axis=1)
    token_mask = jnp.repeat(jnp.repeat(tile_mask, TILE, axis=0), TILE, axis=1)
    scores = jnp.einsum('qhd,khd->hqk', q_rows, key_window) * score_scale
    weights = jnp.where(token_mask[None], jnp.exp(scores - norm_rows[:, :, None]), 0.0)
    weights_half = lax.optimization_barrier(weights.astype(jnp.bfloat16)).astype(jnp.float32)
    prob_grad = jnp.einsum('qhd,khd->hqk', g_rows, value_window)
    score_grad = lax.optimization_barrier((weights * (prob_grad - delta_rows[:, :, None])).astype(jnp.bfloat16)).astype(jnp.float32)
    query_part = jnp.einsum('hqk,khd->qhd', score_grad, key_window) * score_scale
    key_part = jnp.einsum('hqk,qhd->khd', score_grad, q_rows)
    value_part = jnp.einsum('hqk,qhd->khd', weights_half, g_rows)
    return (query_part.reshape(TOK_DEV, HH), key_part.reshape(window_rows, HH), value_part.reshape(window_rows, HH))

def clip_grads(query, key_states, value_states, attn_grad, log_norm, row_delta, tile_lists):
    padding = ((TILE, TILE), (0, 0))
    key_pad = jnp.pad(key_states, padding)
    value_pad = jnp.pad(value_states, padding)
    window_rows = TOK_DEV + 2 * TILE
    empty_acc = jnp.zeros((CLIP_TOK + 2 * TILE, HH), jnp.float32)
    window_row = jnp.arange(window_rows, dtype=jnp.int32)
    is_rim = ((window_row < TILE) | (window_row >= TILE + TOK_DEV))[:, None]

    def cross_round(part):
        rounded = lax.optimization_barrier(part.astype(jnp.bfloat16)).astype(jnp.float32)
        return jnp.where(is_rim, rounded, part)

    def slab_step(totals, slab_index):
        key_acc, value_acc = totals
        query_part, key_part, value_part = slab_terms(query, key_pad, value_pad, attn_grad, log_norm, row_delta, tile_lists, slab_index)
        key_part = cross_round(key_part)
        value_part = cross_round(value_part)
        row_start = (slab_index * TOK_DEV).astype(jnp.int32)
        key_acc = lax.dynamic_update_slice_in_dim(key_acc, lax.dynamic_slice_in_dim(key_acc, row_start, window_rows, 0) + key_part, row_start, 0)
        value_acc = lax.dynamic_update_slice_in_dim(value_acc, lax.dynamic_slice_in_dim(value_acc, row_start, window_rows, 0) + value_part, row_start, 0)
        return ((key_acc, value_acc), query_part.astype(jnp.bfloat16))
    (key_acc, value_acc), query_rows = lax.scan(slab_step, (empty_acc, empty_acc), jnp.arange(N_SEQ, dtype=jnp.int32))
    score_scale = 1.0 / math.sqrt(HD)
    query_grad = query_rows.reshape(CLIP_TOK, HH)
    key_grad = (key_acc[TILE:TILE + CLIP_TOK] * score_scale).astype(jnp.bfloat16)
    value_grad = value_acc[TILE:TILE + CLIP_TOK].astype(jnp.bfloat16)
    return (query_grad, key_grad, value_grad)

def reference(query, key_states, value_states, attn_out, log_norm, out_grad, out_weight, tile_lists):
    flat_out = attn_out.reshape(CLIPS * CLIP_TOK, HH)
    flat_grad = out_grad.reshape(CLIPS * CLIP_TOK, D)
    weight_grad = jnp.dot(flat_out.T, flat_grad, preferred_element_type=jnp.float32)
    attn_grad = jnp.dot(flat_grad, out_weight.T, preferred_element_type=jnp.float32).astype(jnp.bfloat16)
    row_delta = (attn_grad.astype(jnp.float32) * flat_out.astype(jnp.float32)).reshape(CLIPS, CLIP_TOK, HEADS, HD).sum(axis=3)
    row_delta = jnp.transpose(row_delta, (0, 2, 1))
    attn_grad = attn_grad.reshape(CLIPS, CLIP_TOK, HH)

    def one_clip(clip_items):
        return clip_grads(*clip_items)
    query_grad, key_grad, value_grad = lax.map(one_clip, (query, key_states, value_states, attn_grad, log_norm, row_delta, tile_lists))
    return (query_grad, key_grad, value_grad, weight_grad)
```

```python
import functools
import math

import jax
import jax.numpy as jnp
from jax import lax
from jax.experimental import pallas as pl
from jax.experimental.pallas import tpu as pltpu
from jax.sharding import PartitionSpec as P

TILE = 384
HD = 128
VMEM = 56 * 1024 * 1024
NT = (((1,), (1,)), ((), ()))
TN = (((0,), (0,)), ((), ()))


def mm(a, b, dims=(((1,), (0,)), ((), ()))):
    return lax.dot_general(a, b, dims, preferred_element_type=jnp.float32)


def weight_kernel(places, out_ref, grad_ref, part_ref):
    part_ref[0, 0] = mm(out_ref[...], grad_ref[...], TN).astype(part_ref.dtype)


def weight_part(places, rows, grads, send):
    tokens, width = rows.shape
    high = width // 4
    wide = grads.shape[1] // 4

    def out_at(n, p, at):
        swapped = (p % 2) * 2 + p // 2
        return (0, at[0] ^ jnp.where(n == 0, swapped, p))

    def grad_at(n, p, at):
        half = 1 - at[1] if send else at[1]
        return (0, half * 2 + n)

    return pl.pallas_call(
        weight_kernel,
        grid_spec=pltpu.PrefetchScalarGridSpec(
            num_scalar_prefetch=1,
            grid=(2, 4),
            in_specs=[
                pl.BlockSpec((tokens, high), out_at),
                pl.BlockSpec((tokens, wide), grad_at),
            ],
            out_specs=pl.BlockSpec((1, 1, high, wide), lambda n, p, at: (n, p, 0, 0)),
        ),
        out_shape=jax.ShapeDtypeStruct((2, 4, high, wide), jnp.bfloat16),
        compiler_params=pltpu.CompilerParams(vmem_limit_bytes=VMEM),
        cost_estimate=pl.CostEstimate(
            flops=tokens * width * grads.shape[1],
            bytes_accessed=tokens * width * 2 + tokens * grads.shape[1] + width * grads.shape[1],
            transcendentals=0,
        ),
    )(places, rows, grads)


def attend_kernel(scale, halves, chained, places, *refs):
    weights = refs[: 2 if halves else 1]
    refs = refs[len(weights) :]
    (grad_ref, q_ref, o_ref, norm_ref, k_ref, v_ref, kb_ref, vb_ref, ka_ref, va_ref) = refs[:10]
    refs = refs[11:] if chained else refs[10:]
    (dq_ref, dk_ref, dv_ref, low_ref, high_ref) = refs[:5]
    (full, attn_grad, kwin, vwin, kflip, dk, dv) = refs[5:]
    head = pl.program_id(0)
    tokens = q_ref.shape[0]
    tiles = tokens // TILE

    @pl.when(head == 0)
    def _():
        if halves:
            rows = weights[0].shape[0]
            mine = pl.multiple_of(places[1] * rows, rows)
            other = pl.multiple_of((1 - places[1]) * rows, rows)
            full[pl.ds(mine, rows)] = weights[0][...]
            full[pl.ds(other, rows)] = weights[1][...]
            block = full[...]
        else:
            block = weights[0][...]
        got = mm(grad_ref[...], block, NT).astype(jnp.bfloat16)
        for i in range(attn_grad.shape[0]):
            attn_grad[i] = got[:, i * HD : (i + 1) * HD]

    kwin[0] = kb_ref[...]
    vwin[0] = vb_ref[...]
    for t in range(tiles):
        kwin[t + 1] = k_ref[t * TILE : (t + 1) * TILE]
        vwin[t + 1] = v_ref[t * TILE : (t + 1) * TILE]
    kwin[tiles + 1] = ka_ref[...]
    vwin[tiles + 1] = va_ref[...]
    for w in range(tiles + 2):
        kflip[w] = kwin[w].T
    dk[...] = jnp.zeros_like(dk)
    dv[...] = jnp.zeros_like(dv)
    for t in range(tiles):
        rows = slice(t * TILE, (t + 1) * TILE)
        q = q_ref[rows]
        do = attn_grad[head, rows]
        norm = norm_ref[0, :, rows]
        delta = (do.astype(jnp.float32) * o_ref[rows].astype(jnp.float32)).T.sum(0, keepdims=True)
        dq = jnp.zeros((HD, TILE), jnp.float32)
        for n in range(3):
            w = places[2 + t * 3 + n]
            p = jnp.exp(mm(kwin[w], q, NT) * scale - norm)
            ds = (p * (mm(vwin[w], do, NT) - delta)).astype(jnp.bfloat16)
            dv[w] += mm(p.astype(jnp.bfloat16), do)
            dk[w] += mm(ds, q)
            dq += mm(kflip[w], ds)
        dq_ref[rows] = (dq * scale).T.astype(jnp.bfloat16)
    for t in range(tiles):
        rows = slice(t * TILE, (t + 1) * TILE)
        dk_ref[rows] = dk[t + 1]
        dv_ref[rows] = dv[t + 1]
    low_ref[0] = dk[0].astype(jnp.bfloat16)
    low_ref[1] = dv[0].astype(jnp.bfloat16)
    high_ref[0] = dk[tiles + 1].astype(jnp.bfloat16)
    high_ref[1] = dv[tiles + 1].astype(jnp.bfloat16)


def attend(places, step, heads, weights, grads, query, attn_out, norm, keys, values, halos, before):
    tokens, width = query.shape
    tiles = tokens // TILE
    group = heads * HD
    depth = grads.shape[1]

    def at_head(h, at):
        return (0, (at[0] ^ step) * heads + h)

    def column(rows):
        return pl.BlockSpec((rows, HD), at_head)

    whole = [pl.BlockSpec(w.shape, lambda h, at: (0, 0)) for w in (*weights, grads)]
    in_specs = [
        *whole,
        column(tokens),
        column(tokens),
        pl.BlockSpec((1, 1, tokens), lambda h, at: ((at[0] ^ step) * heads + h, 0, 0)),
        column(tokens),
        column(tokens),
        *[column(TILE)] * 4,
    ]
    operands = [*weights, grads, query, attn_out, norm, keys, values, *halos]
    chained = before is not None
    if chained:
        in_specs.append(pl.BlockSpec(memory_space=pl.ANY))
        operands.append(before)
    rim = pl.BlockSpec((2, TILE, HD), lambda h, at: (0, 0, h))
    local = pl.BlockSpec((tokens, HD), lambda h, at: (0, h))
    kept = 3
    return pl.pallas_call(
        functools.partial(attend_kernel, 1.0 / math.sqrt(HD), len(weights) == 2, chained),
        grid_spec=pltpu.PrefetchScalarGridSpec(
            num_scalar_prefetch=1,
            grid=(heads,),
            in_specs=in_specs,
            out_specs=[column(tokens), local, local, rim, rim],
            scratch_shapes=[
                pltpu.VMEM((group, depth), jnp.bfloat16),
                pltpu.VMEM((heads, tokens, HD), jnp.bfloat16),
                pltpu.VMEM((tiles + 2, TILE, HD), jnp.bfloat16),
                pltpu.VMEM((tiles + 2, TILE, HD), jnp.bfloat16),
                pltpu.VMEM((tiles + 2, HD, TILE), jnp.bfloat16),
                pltpu.VMEM((tiles + 2, TILE, HD), jnp.float32),
                pltpu.VMEM((tiles + 2, TILE, HD), jnp.float32),
            ],
        ),
        out_shape=[
            jax.ShapeDtypeStruct((tokens, width), jnp.bfloat16),
            jax.ShapeDtypeStruct((tokens, group), jnp.float32),
            jax.ShapeDtypeStruct((tokens, group), jnp.float32),
            jax.ShapeDtypeStruct((2, TILE, group), jnp.bfloat16),
            jax.ShapeDtypeStruct((2, TILE, group), jnp.bfloat16),
        ],
        input_output_aliases={len(operands): 0} if chained else {},
        compiler_params=pltpu.CompilerParams(vmem_limit_bytes=VMEM),
        cost_estimate=pl.CostEstimate(
            flops=2 * tokens * depth * group + 20 * tokens * kept * TILE * group,
            bytes_accessed=2 * tokens * depth + 2 * depth * group + 24 * tokens * group,
            transcendentals=heads * tokens * kept * TILE,
        ),
    )(places, *operands)


def finish_kernel(scale, chained, places, dk_ref, dv_ref, below_ref, above_ref, *refs):
    key_ref, value_ref = refs[2:] if chained else refs
    tokens = dk_ref.shape[0]
    tiles = tokens // TILE
    for t in range(tiles):
        rows = slice(t * TILE, (t + 1) * TILE)
        key, value = dk_ref[rows], dv_ref[rows]
        if t == 0:
            key = key + below_ref[0].astype(jnp.float32)
            value = value + below_ref[1].astype(jnp.float32)
        if t == tiles - 1:
            key = key + above_ref[0].astype(jnp.float32)
            value = value + above_ref[1].astype(jnp.float32)
        key_ref[rows] = (key * scale).astype(jnp.bfloat16)
        value_ref[rows] = value.astype(jnp.bfloat16)


def finish(places, step, width, dk, dv, below, above, before):
    tokens, group = dk.shape
    chained = before is not None
    parts = group // HD
    local = pl.BlockSpec((tokens, HD), lambda h, at: (0, h))
    rim = pl.BlockSpec((2, TILE, HD), lambda h, at: (0, 0, h))
    placed = pl.BlockSpec((tokens, HD), lambda h, at: (0, (at[0] ^ step) * parts + h))
    in_specs = [local, local, rim, rim]
    operands = [dk, dv, below, above]
    if chained:
        in_specs += [pl.BlockSpec(memory_space=pl.ANY)] * 2
        operands += before
    return pl.pallas_call(
        functools.partial(finish_kernel, 1.0 / math.sqrt(HD), chained),
        grid_spec=pltpu.PrefetchScalarGridSpec(
            num_scalar_prefetch=1, grid=(parts,), in_specs=in_specs, out_specs=[placed, placed]
        ),
        out_shape=[jax.ShapeDtypeStruct((tokens, width), jnp.bfloat16)] * 2,
        input_output_aliases={5: 0, 6: 1} if chained else {},
        compiler_params=pltpu.CompilerParams(vmem_limit_bytes=VMEM),
        cost_estimate=pl.CostEstimate(
            flops=4 * tokens * group, bytes_accessed=16 * tokens * group, transcendentals=0
        ),
    )(places, *operands)


def body(query, key_states, value_states, attn_out, log_norm, out_grad, out_weight, tile_lists):
    dp_size, seq_size = lax.axis_size("dp"), lax.axis_size("seq")
    cube = dp_size == 4 and seq_size == 8
    query, keys, values, rows = query[0], key_states[0], value_states[0], attn_out[0]
    grads = out_grad[0]
    norm = log_norm[0][:, None, :]
    tokens, width = query.shape
    tiles = tokens // TILE
    head_count = norm.shape[0]
    steps = 4
    heads = head_count // steps
    high = width // steps
    dp, seq = lax.axis_index("dp"), lax.axis_index("seq")
    core = seq % 2
    own = lax.dynamic_slice_in_dim(tile_lists[0], seq * tiles, tiles, 0)
    kept = (own - (seq * tiles - 1)).reshape(-1).astype(jnp.int32)
    first = dp if cube else jnp.int32(0)
    places = jnp.concatenate([jnp.stack([first, core]).astype(jnp.int32), kept])

    def swap(value, dp_bit, seq_bit):
        pairs = [
            (a * seq_size + b, (a ^ dp_bit) * seq_size + (b ^ seq_bit))
            for a in range(dp_size)
            for b in range(seq_size)
        ]
        return lax.ppermute(value, ("dp", "seq"), pairs)

    def along(value, by):
        pairs = [(i, i + by) for i in range(seq_size) if 0 <= i + by < seq_size]
        return lax.ppermute(value, "seq", pairs)

    if cube:
        half = lax.dynamic_slice_in_dim(out_weight, core * (high // 2), high // 2, 0)
        by_x, by_y = swap(half, 1, 0), swap(half, 2, 0)
        quarter = high // 4
        by_both = jnp.concatenate([swap(by_x[:quarter], 2, 0), swap(by_y[quarter:], 1, 0)], axis=0)
        blocks = [[out_weight]] + [[b, swap(b, 0, 1)] for b in (by_x, by_y, by_both)]
    else:
        gathered = lax.all_gather(out_weight, "dp", axis=0, tiled=True)
        blocks = [[gathered[i * high : (i + 1) * high]] for i in range(steps)]

    halos = [
        along(keys[tokens - TILE :], 1),
        along(values[tokens - TILE :], 1),
        along(keys[:TILE], -1),
        along(values[:TILE], -1),
    ]

    if cube:
        f32 = jnp.float32
        sent = swap(weight_part(places, rows, grads, True), 0, 1)
        mine = weight_part(places, rows, grads, False)
        total = mine.astype(f32) + sent.astype(f32)
        half = total.astype(jnp.bfloat16)
        over_x = half[0, :2].astype(f32) + swap(half[0, 2:], 1, 0).astype(f32)
        left = over_x[0] + swap(over_x[1].astype(jnp.bfloat16), 2, 0).astype(f32)
        over_y = half[1, :2].astype(f32) + swap(half[1, 2:], 2, 0).astype(f32)
        right = over_y[0] + swap(over_y[1].astype(jnp.bfloat16), 1, 0).astype(f32)
        plane = jnp.concatenate([left, right], axis=1).astype(jnp.bfloat16)

        def cut(value, bit):
            size = value.shape[0] // 2
            mine = lax.dynamic_slice_in_dim(value, bit * size, size, 0)
            other = lax.dynamic_slice_in_dim(value, (1 - bit) * size, size, 0)
            return mine, other

        def join(value, got, bit):
            return jnp.where(
                bit == 0, jnp.concatenate([value, got], 0), jnp.concatenate([got, value], 0)
            )

        low, up = (seq // 2) % 2, seq // 4
        mine, other = cut(plane, low)
        pair = (mine.astype(f32) + swap(other, 0, 2).astype(f32)).astype(jnp.bfloat16)
        mine, other = cut(pair, up)
        line = (mine.astype(f32) + swap(other, 0, 4).astype(f32)).astype(jnp.bfloat16)
        line = join(line, swap(line, 0, 4), up)
        line = join(line, swap(line, 0, 2), low)
        mate = swap(line, 0, 1)
        weight_grad = jnp.where(
            core == 0, jnp.concatenate([line, mate], 1), jnp.concatenate([mate, line], 1)
        ).astype(f32)
    else:
        summed = lax.psum_scatter(
            jnp.einsum("th,td->hd", rows, grads, preferred_element_type=jnp.float32),
            ("dp", "seq"),
            scatter_dimension=0,
            tiled=True,
        )
        weight_grad = lax.all_gather(summed, "seq", axis=0, tiled=True)

    query_grad, done = None, None
    for step in range(steps):
        query_grad, dk, dv, low_rim, high_rim = attend(
            places, step, heads, blocks[step], grads, query, rows, norm, keys, values, halos, query_grad
        )
        below, above = along(high_rim, 1), along(low_rim, -1)
        done = finish(places, step, width, dk, dv, below, above, done)
    return (query_grad[None], done[0][None], done[1][None], weight_grad)


def solution(mesh):
    token = P("dp", "seq", None)
    return jax.shard_map(
        body,
        mesh=mesh,
        in_specs=(token,) * 4
        + (P("dp", None, "seq"), token, P("dp", None), P("dp", None, None)),
        out_specs=(token, token, token, P("dp", None)),
        check_vma=False,
    )
```

```python
import functools
import math

import jax
import jax.numpy as jnp
from jax import lax
from jax.experimental import pallas as pl
from jax.experimental.pallas import tpu as pltpu
from jax.sharding import PartitionSpec as P

TILE = 384
HD = 128
VMEM = 56 * 1024 * 1024
NT = (((1,), (1,)), ((), ()))
TN = (((0,), (0,)), ((), ()))


def mm(a, b, dims=(((1,), (0,)), ((), ()))):
    return lax.dot_general(a, b, dims, preferred_element_type=jnp.float32)


def weight_kernel(places, out_ref, grad_ref, part_ref):
    part_ref[0] = mm(out_ref[...], grad_ref[...], TN).astype(part_ref.dtype)


def weight_part(places, rows, grads, send):
    tokens, width = rows.shape
    high = width // 4
    wide = grads.shape[1] // 2

    def half(at):
        return 1 - at[1] if send else at[1]

    def out_at(p, at):
        swapped = (p % 2) * 2 + p // 2
        return (0, at[0] ^ jnp.where(half(at) == 0, swapped, p))

    return pl.pallas_call(
        weight_kernel,
        grid_spec=pltpu.PrefetchScalarGridSpec(
            num_scalar_prefetch=1,
            grid=(4,),
            in_specs=[
                pl.BlockSpec((tokens, high), out_at),
                pl.BlockSpec((tokens, wide), lambda p, at: (0, half(at))),
            ],
            out_specs=pl.BlockSpec((1, high, wide), lambda p, at: (p, 0, 0)),
        ),
        out_shape=jax.ShapeDtypeStruct((4, high, wide), jnp.bfloat16),
        compiler_params=pltpu.CompilerParams(vmem_limit_bytes=VMEM),
        cost_estimate=pl.CostEstimate(
            flops=tokens * width * grads.shape[1],
            bytes_accessed=tokens * width * 2 + tokens * grads.shape[1] + width * grads.shape[1],
            transcendentals=0,
        ),
    )(places, rows, grads)


def sum_kernel(count, places, *refs):
    a0, b0, a1, b1 = refs[:4]
    keep_ref, send_ref = refs[4 + count :]
    f32 = jnp.float32
    keep_ref[...] = (a0[...].astype(f32) + b0[...].astype(f32)).astype(jnp.bfloat16)
    send_ref[...] = (a1[...].astype(f32) + b1[...].astype(f32)).astype(jnp.bfloat16)


def line_kernel(count, places, a_ref, b_ref, *refs):
    f32 = jnp.float32
    refs[count][...] = (a_ref[...].astype(f32) + b_ref[...].astype(f32)).astype(jnp.bfloat16)


def sum_whole(places, a, b, after):
    whole = pl.BlockSpec(a.shape, lambda i, at: (0, 0))
    return pl.pallas_call(
        functools.partial(line_kernel, len(after)),
        grid_spec=pltpu.PrefetchScalarGridSpec(
            num_scalar_prefetch=1,
            grid=(1,),
            in_specs=[whole, whole] + [pl.BlockSpec(memory_space=pl.ANY)] * len(after),
            out_specs=whole,
        ),
        out_shape=jax.ShapeDtypeStruct(a.shape, jnp.bfloat16),
        compiler_params=pltpu.CompilerParams(vmem_limit_bytes=VMEM),
        cost_estimate=pl.CostEstimate(
            flops=a.size, bytes_accessed=6 * a.size, transcendentals=0
        ),
    )(places, a, b, *after)


def sum_and_cut(places, bit, a, b, after=()):
    size, wide = a.shape[0] // 2, a.shape[1]
    chunk = min(size, 192)
    steps = size // chunk

    def half(at):
        return 0 if bit is None else at[bit]

    kept = pl.BlockSpec((chunk, wide), lambda i, at: (half(at) * steps + i, 0))
    sent = pl.BlockSpec((chunk, wide), lambda i, at: ((1 - half(at)) * steps + i, 0))
    out = pl.BlockSpec((chunk, wide), lambda i, at: (i, 0))
    return pl.pallas_call(
        functools.partial(sum_kernel, len(after)),
        grid_spec=pltpu.PrefetchScalarGridSpec(
            num_scalar_prefetch=1,
            grid=(steps,),
            in_specs=[kept, kept, sent, sent] + [pl.BlockSpec(memory_space=pl.ANY)] * len(after),
            out_specs=[out, out],
        ),
        out_shape=[jax.ShapeDtypeStruct((size, wide), jnp.bfloat16)] * 2,
        compiler_params=pltpu.CompilerParams(vmem_limit_bytes=VMEM),
        cost_estimate=pl.CostEstimate(
            flops=a.size, bytes_accessed=6 * a.size, transcendentals=0
        ),
    )(places, a, b, a, b, *after)


def attend_kernel(scale, halves, extra, places, *refs):
    weights = refs[: 2 if halves else 1]
    refs = refs[len(weights) :]
    (grad_ref, q_ref, o_ref, norm_ref, k_ref, v_ref, below_ref, above_ref) = refs[:8]
    refs = refs[8 + extra :]
    (dq_ref, dk_ref, dv_ref, low_ref, high_ref) = refs[:5]
    (full, attn_grad, kwin, vwin, kflip, dk, dv) = refs[5:]
    head = pl.program_id(0)
    tokens = q_ref.shape[0]
    tiles = tokens // TILE

    @pl.when(head == 0)
    def _():
        if halves:
            rows = weights[0].shape[0]
            mine = pl.multiple_of(places[1] * rows, rows)
            other = pl.multiple_of((1 - places[1]) * rows, rows)
            full[pl.ds(mine, rows)] = weights[0][...]
            full[pl.ds(other, rows)] = weights[1][...]
            block = full[...]
        else:
            block = weights[0][...]
        got = mm(grad_ref[...], block, NT).astype(jnp.bfloat16)
        for i in range(attn_grad.shape[0]):
            attn_grad[i] = got[:, i * HD : (i + 1) * HD]

    kwin[0] = below_ref[0]
    vwin[0] = below_ref[1]
    for t in range(tiles):
        kwin[t + 1] = k_ref[t * TILE : (t + 1) * TILE]
        vwin[t + 1] = v_ref[t * TILE : (t + 1) * TILE]
    kwin[tiles + 1] = above_ref[0]
    vwin[tiles + 1] = above_ref[1]
    for w in range(tiles + 2):
        kflip[w] = kwin[w].T
    dk[...] = jnp.zeros_like(dk)
    dv[...] = jnp.zeros_like(dv)
    log2e = 1.0 / math.log(2.0)

    def rows_of(t):
        return slice(t * TILE, (t + 1) * TILE)

    def products(t, n):
        w = places[4 + t * 3 + n]
        q, do = q_ref[rows_of(t)], attn_grad[head, rows_of(t)]
        return w, mm(kwin[w], q, NT), mm(vwin[w], do, NT)

    pieces = [(t, n) for t in range(tiles) for n in range(3)]
    ahead = products(*pieces[0])
    dq = None
    for at, (t, n) in enumerate(pieces):
        w, scores, prob = ahead
        if at + 1 < len(pieces):
            ahead = products(*pieces[at + 1])
        rows = rows_of(t)
        q, do = q_ref[rows], attn_grad[head, rows]
        if n == 0:
            norm = norm_ref[0, :, rows] * log2e
            both = do.astype(jnp.float32) * o_ref[rows].astype(jnp.float32)
            delta = both.T.sum(0, keepdims=True)
        p = jnp.exp2(scores * (scale * log2e) - norm)
        ds = (p * (prob - delta)).astype(jnp.bfloat16)
        dv[w] += mm(p.astype(jnp.bfloat16), do)
        dk[w] += mm(ds, q)
        part = mm(kflip[w], ds)
        dq = part if n == 0 else dq + part
        if n == 2:
            dq_ref[rows] = (dq * scale).T.astype(jnp.bfloat16)
    for t in range(tiles):
        dk_ref[rows_of(t)] = dk[t + 1].astype(jnp.bfloat16)
        dv_ref[rows_of(t)] = dv[t + 1].astype(jnp.bfloat16)
    low_ref[0] = dk[0].astype(jnp.bfloat16)
    low_ref[1] = dv[0].astype(jnp.bfloat16)
    high_ref[0] = dk[tiles + 1].astype(jnp.bfloat16)
    high_ref[1] = dv[tiles + 1].astype(jnp.bfloat16)


def attend(places, step, heads, weights, grads, query, attn_out, norm, keys, values, halos, before, after=()):
    tokens, width = query.shape
    tiles = tokens // TILE
    group = heads * HD
    depth = grads.shape[1]

    def at_head(h, at):
        return (0, (at[0] ^ step) * heads + h)

    def column(rows):
        return pl.BlockSpec((rows, HD), at_head)

    whole = [pl.BlockSpec(w.shape, lambda h, at: (0, 0)) for w in (*weights, grads)]
    in_specs = [
        *whole,
        column(tokens),
        column(tokens),
        pl.BlockSpec((1, 1, tokens), lambda h, at: ((at[0] ^ step) * heads + h, 0, 0)),
        column(tokens),
        column(tokens),
        *[pl.BlockSpec((2, TILE, HD), lambda h, at: (0, 0, (at[0] ^ step) * heads + h))] * 2,
    ]
    operands = [*weights, grads, query, attn_out, norm, keys, values, *halos]
    aliases = {}
    if before is not None:
        aliases = {len(operands) + 1 + i: i for i in range(3)}
        operands += before
    operands += after
    extra = len(operands) - len(in_specs)
    in_specs += [pl.BlockSpec(memory_space=pl.ANY)] * extra
    rim = pl.BlockSpec((2, TILE, HD), lambda h, at: (0, 0, h))
    kept = 3
    return pl.pallas_call(
        functools.partial(attend_kernel, 1.0 / math.sqrt(HD), len(weights) == 2, extra),
        grid_spec=pltpu.PrefetchScalarGridSpec(
            num_scalar_prefetch=1,
            grid=(heads,),
            in_specs=in_specs,
            out_specs=[column(tokens)] * 3 + [rim, rim],
            scratch_shapes=[
                pltpu.VMEM((group, depth), jnp.bfloat16),
                pltpu.VMEM((heads, tokens, HD), jnp.bfloat16),
                pltpu.VMEM((tiles + 2, TILE, HD), jnp.bfloat16),
                pltpu.VMEM((tiles + 2, TILE, HD), jnp.bfloat16),
                pltpu.VMEM((tiles + 2, HD, TILE), jnp.bfloat16),
                pltpu.VMEM((tiles + 2, TILE, HD), jnp.float32),
                pltpu.VMEM((tiles + 2, TILE, HD), jnp.float32),
            ],
        ),
        out_shape=[
            *[jax.ShapeDtypeStruct((tokens, width), jnp.bfloat16)] * 3,
            jax.ShapeDtypeStruct((2, TILE, group), jnp.bfloat16),
            jax.ShapeDtypeStruct((2, TILE, group), jnp.bfloat16),
        ],
        input_output_aliases=aliases,
        compiler_params=pltpu.CompilerParams(vmem_limit_bytes=VMEM),
        cost_estimate=pl.CostEstimate(
            flops=2 * tokens * depth * group + 20 * tokens * kept * TILE * group,
            bytes_accessed=2 * tokens * depth + 2 * depth * group + 24 * tokens * group,
            transcendentals=heads * tokens * kept * TILE,
        ),
    )(places, *operands)


def finish_kernel(scale, places, dk_ref, dv_ref, *refs):
    rims, (key_ref, value_ref) = refs[:-2], refs[-2:]
    tokens = dk_ref.shape[0]
    tiles = tokens // TILE
    f32 = jnp.float32
    for step in range(len(rims) // 2):

        @pl.when(pl.program_id(0) == step)
        def _(below=rims[2 * step], above=rims[2 * step + 1]):
            for t in range(tiles):
                rows = slice(t * TILE, (t + 1) * TILE)
                key, value = dk_ref[rows].astype(f32), dv_ref[rows].astype(f32)
                if t == 0:
                    key, value = key + below[0].astype(f32), value + below[1].astype(f32)
                if t == tiles - 1:
                    key, value = key + above[0].astype(f32), value + above[1].astype(f32)
                key_ref[rows] = (key * scale).astype(jnp.bfloat16)
                value_ref[rows] = value.astype(jnp.bfloat16)


def finish(places, dk, dv, rims):
    tokens, width = dk.shape
    steps = len(rims) // 2
    group = width // steps
    rim = pl.BlockSpec((2, TILE, group), lambda j, at: (0, 0, 0))
    placed = pl.BlockSpec((tokens, group), lambda j, at: (0, at[0] ^ j))
    return pl.pallas_call(
        functools.partial(finish_kernel, 1.0 / math.sqrt(HD)),
        grid_spec=pltpu.PrefetchScalarGridSpec(
            num_scalar_prefetch=1,
            grid=(steps,),
            in_specs=[placed, placed] + [rim] * len(rims),
            out_specs=[placed, placed],
        ),
        out_shape=[jax.ShapeDtypeStruct((tokens, width), jnp.bfloat16)] * 2,
        compiler_params=pltpu.CompilerParams(vmem_limit_bytes=VMEM),
        cost_estimate=pl.CostEstimate(
            flops=4 * tokens * width, bytes_accessed=12 * tokens * width, transcendentals=0
        ),
    )(places, dk, dv, *rims)


def body(query, key_states, value_states, attn_out, log_norm, out_grad, out_weight, tile_lists):
    dp_size, seq_size = lax.axis_size("dp"), lax.axis_size("seq")
    cube = dp_size == 4 and seq_size == 8
    query, keys, values, rows = query[0], key_states[0], value_states[0], attn_out[0]
    grads = out_grad[0]
    norm = log_norm[0][:, None, :]
    tokens, width = query.shape
    tiles = tokens // TILE
    head_count = norm.shape[0]
    steps = 4
    heads = head_count // steps
    high = width // steps
    dp, seq = lax.axis_index("dp"), lax.axis_index("seq")
    core = seq % 2
    own = lax.dynamic_slice_in_dim(tile_lists[0], seq * tiles, tiles, 0)
    kept = (own - (seq * tiles - 1)).reshape(-1).astype(jnp.int32)
    first = dp if cube else jnp.int32(0)
    bits = jnp.stack([first, core, (seq // 2) % 2, seq // 4]).astype(jnp.int32)
    places = jnp.concatenate([bits, kept])

    def send(value, partner):
        pairs = []
        for a in range(dp_size):
            for b in range(seq_size):
                to, at = partner(a, b)
                pairs.append((a * seq_size + b, to * seq_size + at))
        return lax.ppermute(value, ("dp", "seq"), pairs)

    def swap(value, dp_bit, seq_bit):
        return send(value, lambda a, b: (a ^ dp_bit, b ^ seq_bit))

    def swap_by_core(value, bits):
        return send(value, lambda a, b: (a ^ bits[b % 2], b))

    def along(value, by):
        pairs = [(i, i + by) for i in range(seq_size) if 0 <= i + by < seq_size]
        return lax.ppermute(value, "seq", pairs)

    if cube:
        half = lax.dynamic_slice_in_dim(out_weight, core * (high // 2), high // 2, 0)
        by_x, by_y = swap(half, 1, 0), swap(half, 2, 0)
        by_both = swap_by_core(jnp.where(core == 0, by_x, by_y), (2, 1))
        blocks = [[out_weight]] + [[b, swap(b, 0, 1)] for b in (by_x, by_y, by_both)]
    else:
        gathered = lax.all_gather(out_weight, "dp", axis=0, tiled=True)
        blocks = [[gathered[i * high : (i + 1) * high]] for i in range(steps)]

    halos = [
        along(jnp.stack([keys[tokens - TILE :], values[tokens - TILE :]]), 1),
        along(jnp.stack([keys[:TILE], values[:TILE]]), -1),
    ]

    first_after = ()
    if cube:
        wide = grads.shape[1] // 2
        sent = swap(weight_part(places, rows, grads, True), 0, 1).reshape(width, wide)
        mine = weight_part(places, rows, grads, False).reshape(width, wide)
        chip_keep, chip_send = sum_and_cut(places, None, mine, sent)
        chip_got = swap_by_core(chip_send, (1, 2))
        first_after = (chip_send,)

    results, rims, marks = None, [], []
    for step in range(steps):
        after = first_after if step == 0 else rims[2 * step - 4 : 2 * step - 2] if step > 1 else ()
        *results, low_rim, high_rim = attend(
            places, step, heads, blocks[step], grads, query, rows, norm, keys, values, halos, results, after
        )
        rims += [along(high_rim, 1), along(low_rim, -1)]
        marks.append((low_rim,))
    key_grad, value_grad = finish(places, results[1], results[2], rims)

    if cube:

        def join(value, got, bit):
            return jnp.where(
                bit == 0, jnp.concatenate([value, got], 0), jnp.concatenate([got, value], 0)
            )

        keep, other = sum_and_cut(places, None, chip_keep, chip_got)
        keep, other = sum_and_cut(places, 2, keep, swap_by_core(other, (2, 1)), marks[0])
        keep, other = sum_and_cut(places, 3, keep, swap(other, 0, 2), marks[1])
        line = sum_whole(places, keep, swap(other, 0, 4), marks[2])
        line = join(line, swap(line, 0, 4), places[3])
        line = join(line, swap(line, 0, 2), places[2])
        mate = swap(line, 0, 1)
        weight_grad = jnp.where(
            core == 0, jnp.concatenate([line, mate], 1), jnp.concatenate([mate, line], 1)
        ).astype(jnp.float32)
    else:
        summed = lax.psum_scatter(
            jnp.einsum("th,td->hd", rows, grads, preferred_element_type=jnp.float32),
            ("dp", "seq"),
            scatter_dimension=0,
            tiled=True,
        )
        weight_grad = lax.all_gather(summed, "seq", axis=0, tiled=True)
    return (results[0][None], key_grad[None], value_grad[None], weight_grad)


def solution(mesh):
    token = P("dp", "seq", None)
    return jax.shard_map(
        body,
        mesh=mesh,
        in_specs=(token,) * 4
        + (P("dp", None, "seq"), token, P("dp", None), P("dp", None, None)),
        out_specs=(token, token, token, P("dp", None)),
        check_vma=False,
    )
```

```python
import functools
import math

import jax
import jax.numpy as jnp
from jax import lax
from jax.experimental import pallas as pl
from jax.experimental.pallas import tpu as pltpu
from jax.sharding import PartitionSpec as P

TILE = 384
HD = 128
VMEM = 56 * 1024 * 1024
NT = (((1,), (1,)), ((), ()))
TN = (((0,), (0,)), ((), ()))


def mm(a, b, dims=(((1,), (0,)), ((), ()))):
    return lax.dot_general(a, b, dims, preferred_element_type=jnp.float32)


def weight_kernel(places, out_ref, grad_ref, part_ref):
    part_ref[0] = mm(out_ref[...], grad_ref[...], TN).astype(part_ref.dtype)


def weight_part(places, rows, grads, send):
    tokens, width = rows.shape
    high = width // 4
    wide = grads.shape[1] // 2

    def half(at):
        return 1 - at[1] if send else at[1]

    def out_at(p, at):
        swapped = (p % 2) * 2 + p // 2
        return (0, at[0] ^ jnp.where(half(at) == 0, swapped, p))

    return pl.pallas_call(
        weight_kernel,
        grid_spec=pltpu.PrefetchScalarGridSpec(
            num_scalar_prefetch=1,
            grid=(4,),
            in_specs=[
                pl.BlockSpec((tokens, high), out_at),
                pl.BlockSpec((tokens, wide), lambda p, at: (0, half(at))),
            ],
            out_specs=pl.BlockSpec((1, high, wide), lambda p, at: (p, 0, 0)),
        ),
        out_shape=jax.ShapeDtypeStruct((4, high, wide), jnp.bfloat16),
        compiler_params=pltpu.CompilerParams(vmem_limit_bytes=VMEM),
        cost_estimate=pl.CostEstimate(
            flops=tokens * width * grads.shape[1],
            bytes_accessed=tokens * width * 2 + tokens * grads.shape[1] + width * grads.shape[1],
            transcendentals=0,
        ),
    )(places, rows, grads)


def sum_kernel(count, places, *refs):
    a0, b0, a1, b1 = refs[:4]
    keep_ref, send_ref = refs[4 + count :]
    f32 = jnp.float32
    keep_ref[...] = (a0[...].astype(f32) + b0[...].astype(f32)).astype(jnp.bfloat16)
    send_ref[...] = (a1[...].astype(f32) + b1[...].astype(f32)).astype(jnp.bfloat16)


def line_kernel(count, places, a_ref, b_ref, *refs):
    f32 = jnp.float32
    refs[count][...] = (a_ref[...].astype(f32) + b_ref[...].astype(f32)).astype(jnp.bfloat16)


def sum_whole(places, a, b, after):
    whole = pl.BlockSpec(a.shape, lambda i, at: (0, 0))
    return pl.pallas_call(
        functools.partial(line_kernel, len(after)),
        grid_spec=pltpu.PrefetchScalarGridSpec(
            num_scalar_prefetch=1,
            grid=(1,),
            in_specs=[whole, whole] + [pl.BlockSpec(memory_space=pl.ANY)] * len(after),
            out_specs=whole,
        ),
        out_shape=jax.ShapeDtypeStruct(a.shape, jnp.bfloat16),
        compiler_params=pltpu.CompilerParams(vmem_limit_bytes=VMEM),
        cost_estimate=pl.CostEstimate(
            flops=a.size, bytes_accessed=6 * a.size, transcendentals=0
        ),
    )(places, a, b, *after)


def join_kernel(bit, count, places, mine_ref, other_ref, *refs):
    rows = mine_ref.shape[0]
    at = places[bit]
    refs[count][pl.ds(pl.multiple_of(at * rows, rows), rows)] = mine_ref[...]
    refs[count][pl.ds(pl.multiple_of((1 - at) * rows, rows), rows)] = other_ref[...]


def join(places, bit, mine, other, after):
    rows, wide = mine.shape
    whole = pl.BlockSpec((rows, wide), lambda i, at: (0, 0))
    return pl.pallas_call(
        functools.partial(join_kernel, bit, len(after)),
        grid_spec=pltpu.PrefetchScalarGridSpec(
            num_scalar_prefetch=1,
            grid=(1,),
            in_specs=[whole, whole] + [pl.BlockSpec(memory_space=pl.ANY)] * len(after),
            out_specs=pl.BlockSpec((2 * rows, wide), lambda i, at: (0, 0)),
        ),
        out_shape=jax.ShapeDtypeStruct((2 * rows, wide), mine.dtype),
        compiler_params=pltpu.CompilerParams(vmem_limit_bytes=VMEM),
        cost_estimate=pl.CostEstimate(
            flops=mine.size, bytes_accessed=8 * mine.size, transcendentals=0
        ),
    )(places, mine, other, *after)


def sum_and_cut(places, bit, a, b, after=()):
    size, wide = a.shape[0] // 2, a.shape[1]
    chunk = min(size, 192)
    steps = size // chunk

    def half(at):
        return 0 if bit is None else at[bit]

    kept = pl.BlockSpec((chunk, wide), lambda i, at: (half(at) * steps + i, 0))
    sent = pl.BlockSpec((chunk, wide), lambda i, at: ((1 - half(at)) * steps + i, 0))
    out = pl.BlockSpec((chunk, wide), lambda i, at: (i, 0))
    return pl.pallas_call(
        functools.partial(sum_kernel, len(after)),
        grid_spec=pltpu.PrefetchScalarGridSpec(
            num_scalar_prefetch=1,
            grid=(steps,),
            in_specs=[kept, kept, sent, sent] + [pl.BlockSpec(memory_space=pl.ANY)] * len(after),
            out_specs=[out, out],
        ),
        out_shape=[jax.ShapeDtypeStruct((size, wide), jnp.bfloat16)] * 2,
        compiler_params=pltpu.CompilerParams(vmem_limit_bytes=VMEM),
        cost_estimate=pl.CostEstimate(
            flops=a.size, bytes_accessed=6 * a.size, transcendentals=0
        ),
    )(places, a, b, a, b, *after)


def attend_kernel(scale, halves, extra, places, *refs):
    weights = refs[: 2 if halves else 1]
    refs = refs[len(weights) :]
    (grad_ref, q_ref, o_ref, norm_ref, k_ref, v_ref, below_ref, above_ref) = refs[:8]
    refs = refs[8 + extra :]
    (dq_ref, dk_ref, dv_ref, low_ref, high_ref) = refs[:5]
    (full, attn_grad, kwin, vwin, kflip, kcat, vcat, fcat, dk, dv) = refs[5:]
    head = pl.program_id(0)
    tokens = q_ref.shape[0]
    tiles = tokens // TILE

    @pl.when(head == 0)
    def _():
        if halves:
            rows = weights[0].shape[0]
            mine = pl.multiple_of(places[1] * rows, rows)
            other = pl.multiple_of((1 - places[1]) * rows, rows)
            full[pl.ds(mine, rows)] = weights[0][...]
            full[pl.ds(other, rows)] = weights[1][...]
            block = full[...]
        else:
            block = weights[0][...]
        got = mm(grad_ref[...], block, NT).astype(jnp.bfloat16)
        for i in range(attn_grad.shape[0]):
            attn_grad[i] = got[:, i * HD : (i + 1) * HD]

    kwin[0] = below_ref[0]
    vwin[0] = below_ref[1]
    for t in range(tiles):
        kwin[t + 1] = k_ref[t * TILE : (t + 1) * TILE]
        vwin[t + 1] = v_ref[t * TILE : (t + 1) * TILE]
    kwin[tiles + 1] = above_ref[0]
    vwin[tiles + 1] = above_ref[1]
    for w in range(tiles + 2):
        kflip[w] = kwin[w].T
    dk[...] = jnp.zeros_like(dk)
    dv[...] = jnp.zeros_like(dv)
    log2e = 1.0 / math.log(2.0)

    def rows_of(t):
        return slice(t * TILE, (t + 1) * TILE)

    def products(t):
        kept = [places[4 + t * 3 + n] for n in range(3)]
        for n, w in enumerate(kept):
            part = slice(n * TILE, (n + 1) * TILE)
            kcat[t, part] = kwin[w]
            vcat[t, part] = vwin[w]
            fcat[t, :, part] = kflip[w]
        q, do = q_ref[rows_of(t)], attn_grad[head, rows_of(t)]
        return kept, mm(kcat[t], q, NT), mm(vcat[t], do, NT)

    ahead = products(0)
    for t in range(tiles):
        kept, scores, prob = ahead
        if t + 1 < tiles:
            ahead = products(t + 1)
        rows = rows_of(t)
        q, do = q_ref[rows], attn_grad[head, rows]
        norm = norm_ref[0, :, rows] * log2e
        both = do.astype(jnp.float32) * o_ref[rows].astype(jnp.float32)
        delta = both.T.sum(0, keepdims=True)
        p = jnp.exp2(scores * (scale * log2e) - norm)
        ds = (p * (prob - delta)).astype(jnp.bfloat16)
        dv_all = mm(p.astype(jnp.bfloat16), do)
        dk_all = mm(ds, q)
        dq_ref[rows] = (mm(fcat[t], ds) * scale).T.astype(jnp.bfloat16)
        for n, w in enumerate(kept):
            part = slice(n * TILE, (n + 1) * TILE)
            dv[w] += dv_all[part]
            dk[w] += dk_all[part]
    for t in range(tiles):
        dk_ref[rows_of(t)] = dk[t + 1].astype(jnp.bfloat16)
        dv_ref[rows_of(t)] = dv[t + 1].astype(jnp.bfloat16)
    low_ref[0] = dk[0].astype(jnp.bfloat16)
    low_ref[1] = dv[0].astype(jnp.bfloat16)
    high_ref[0] = dk[tiles + 1].astype(jnp.bfloat16)
    high_ref[1] = dv[tiles + 1].astype(jnp.bfloat16)


def attend(places, step, heads, weights, grads, query, attn_out, norm, keys, values, halos, before, after=()):
    tokens, width = query.shape
    tiles = tokens // TILE
    group = heads * HD
    depth = grads.shape[1]

    def at_head(h, at):
        return (0, (at[0] ^ step) * heads + h)

    def column(rows):
        return pl.BlockSpec((rows, HD), at_head)

    whole = [pl.BlockSpec(w.shape, lambda h, at: (0, 0)) for w in (*weights, grads)]
    in_specs = [
        *whole,
        column(tokens),
        column(tokens),
        pl.BlockSpec((1, 1, tokens), lambda h, at: ((at[0] ^ step) * heads + h, 0, 0)),
        column(tokens),
        column(tokens),
        *[pl.BlockSpec((2, TILE, HD), lambda h, at: (0, 0, (at[0] ^ step) * heads + h))] * 2,
    ]
    operands = [*weights, grads, query, attn_out, norm, keys, values, *halos]
    aliases = {}
    if before is not None:
        aliases = {len(operands) + 1 + i: i for i in range(3)}
        operands += before
    operands += after
    extra = len(operands) - len(in_specs)
    in_specs += [pl.BlockSpec(memory_space=pl.ANY)] * extra
    rim = pl.BlockSpec((2, TILE, HD), lambda h, at: (0, 0, h))
    kept = 3
    return pl.pallas_call(
        functools.partial(attend_kernel, 1.0 / math.sqrt(HD), len(weights) == 2, extra),
        grid_spec=pltpu.PrefetchScalarGridSpec(
            num_scalar_prefetch=1,
            grid=(heads,),
            in_specs=in_specs,
            out_specs=[column(tokens)] * 3 + [rim, rim],
            scratch_shapes=[
                pltpu.VMEM((group, depth), jnp.bfloat16),
                pltpu.VMEM((heads, tokens, HD), jnp.bfloat16),
                pltpu.VMEM((tiles + 2, TILE, HD), jnp.bfloat16),
                pltpu.VMEM((tiles + 2, TILE, HD), jnp.bfloat16),
                pltpu.VMEM((tiles + 2, HD, TILE), jnp.bfloat16),
                pltpu.VMEM((tiles, kept * TILE, HD), jnp.bfloat16),
                pltpu.VMEM((tiles, kept * TILE, HD), jnp.bfloat16),
                pltpu.VMEM((tiles, HD, kept * TILE), jnp.bfloat16),
                pltpu.VMEM((tiles + 2, TILE, HD), jnp.float32),
                pltpu.VMEM((tiles + 2, TILE, HD), jnp.float32),
            ],
        ),
        out_shape=[
            *[jax.ShapeDtypeStruct((tokens, width), jnp.bfloat16)] * 3,
            jax.ShapeDtypeStruct((2, TILE, group), jnp.bfloat16),
            jax.ShapeDtypeStruct((2, TILE, group), jnp.bfloat16),
        ],
        input_output_aliases=aliases,
        compiler_params=pltpu.CompilerParams(vmem_limit_bytes=VMEM),
        cost_estimate=pl.CostEstimate(
            flops=2 * tokens * depth * group + 20 * tokens * kept * TILE * group,
            bytes_accessed=2 * tokens * depth + 2 * depth * group + 24 * tokens * group,
            transcendentals=heads * tokens * kept * TILE,
        ),
    )(places, *operands)


def finish_kernel(scale, places, dk_ref, dv_ref, *refs):
    rims, (key_ref, value_ref) = refs[:-2], refs[-2:]
    tokens = dk_ref.shape[0]
    tiles = tokens // TILE
    f32 = jnp.float32
    for step in range(len(rims) // 2):

        @pl.when(pl.program_id(0) == step)
        def _(below=rims[2 * step], above=rims[2 * step + 1]):
            for t in range(tiles):
                rows = slice(t * TILE, (t + 1) * TILE)
                key, value = dk_ref[rows].astype(f32), dv_ref[rows].astype(f32)
                if t == 0:
                    key, value = key + below[0].astype(f32), value + below[1].astype(f32)
                if t == tiles - 1:
                    key, value = key + above[0].astype(f32), value + above[1].astype(f32)
                key_ref[rows] = (key * scale).astype(jnp.bfloat16)
                value_ref[rows] = value.astype(jnp.bfloat16)


def finish(places, dk, dv, rims):
    tokens, width = dk.shape
    steps = len(rims) // 2
    group = width // steps
    rim = pl.BlockSpec((2, TILE, group), lambda j, at: (0, 0, 0))
    placed = pl.BlockSpec((tokens, group), lambda j, at: (0, at[0] ^ j))
    return pl.pallas_call(
        functools.partial(finish_kernel, 1.0 / math.sqrt(HD)),
        grid_spec=pltpu.PrefetchScalarGridSpec(
            num_scalar_prefetch=1,
            grid=(steps,),
            in_specs=[placed, placed] + [rim] * len(rims),
            out_specs=[placed, placed],
        ),
        out_shape=[jax.ShapeDtypeStruct((tokens, width), jnp.bfloat16)] * 2,
        compiler_params=pltpu.CompilerParams(vmem_limit_bytes=VMEM),
        cost_estimate=pl.CostEstimate(
            flops=4 * tokens * width, bytes_accessed=12 * tokens * width, transcendentals=0
        ),
    )(places, dk, dv, *rims)


def body(query, key_states, value_states, attn_out, log_norm, out_grad, out_weight, tile_lists):
    dp_size, seq_size = lax.axis_size("dp"), lax.axis_size("seq")
    cube = dp_size == 4 and seq_size == 8
    query, keys, values, rows = query[0], key_states[0], value_states[0], attn_out[0]
    grads = out_grad[0]
    norm = log_norm[0][:, None, :]
    tokens, width = query.shape
    tiles = tokens // TILE
    head_count = norm.shape[0]
    steps = 4
    heads = head_count // steps
    high = width // steps
    dp, seq = lax.axis_index("dp"), lax.axis_index("seq")
    core = seq % 2
    own = lax.dynamic_slice_in_dim(tile_lists[0], seq * tiles, tiles, 0)
    kept = (own - (seq * tiles - 1)).reshape(-1).astype(jnp.int32)
    first = dp if cube else jnp.int32(0)
    bits = jnp.stack([first, core, (seq // 2) % 2, seq // 4]).astype(jnp.int32)
    places = jnp.concatenate([bits, kept])

    def send(value, partner):
        pairs = []
        for a in range(dp_size):
            for b in range(seq_size):
                to, at = partner(a, b)
                pairs.append((a * seq_size + b, to * seq_size + at))
        return lax.ppermute(value, ("dp", "seq"), pairs)

    def swap(value, dp_bit, seq_bit):
        return send(value, lambda a, b: (a ^ dp_bit, b ^ seq_bit))

    def swap_by_core(value, bits):
        return send(value, lambda a, b: (a ^ bits[b % 2], b))

    def along(value, by):
        pairs = [(i, i + by) for i in range(seq_size) if 0 <= i + by < seq_size]
        return lax.ppermute(value, "seq", pairs)

    if cube:
        half = lax.dynamic_slice_in_dim(out_weight, core * (high // 2), high // 2, 0)
        by_x, by_y = swap(half, 1, 0), swap(half, 2, 0)
        by_both = swap_by_core(jnp.where(core == 0, by_x, by_y), (2, 1))
        blocks = [[out_weight]] + [[b, swap(b, 0, 1)] for b in (by_x, by_y, by_both)]
    else:
        gathered = lax.all_gather(out_weight, "dp", axis=0, tiled=True)
        blocks = [[gathered[i * high : (i + 1) * high]] for i in range(steps)]

    halos = [
        along(jnp.stack([keys[tokens - TILE :], values[tokens - TILE :]]), 1),
        along(jnp.stack([keys[:TILE], values[:TILE]]), -1),
    ]

    first_after = ()
    if cube:
        wide = grads.shape[1] // 2
        sent = swap(weight_part(places, rows, grads, True), 0, 1).reshape(width, wide)
        mine = weight_part(places, rows, grads, False).reshape(width, wide)
        chip_keep, chip_send = sum_and_cut(places, None, mine, sent, (by_x, by_y, *halos))
        chip_got = swap_by_core(chip_send, (1, 2))
        first_after = (chip_send,)

    results, rims, marks = None, [], []
    for step in range(steps):
        after = first_after if step == 0 else rims[2 * step - 4 : 2 * step - 2] if step > 1 else ()
        *results, low_rim, high_rim = attend(
            places, step, heads, blocks[step], grads, query, rows, norm, keys, values, halos, results, after
        )
        rims += [along(high_rim, 1), along(low_rim, -1)]
        marks.append((low_rim,))
    key_grad, value_grad = finish(places, results[1], results[2], rims)

    if cube:
        keep, other = sum_and_cut(places, None, chip_keep, chip_got, marks[0])
        keep, other = sum_and_cut(places, 2, keep, swap_by_core(other, (2, 1)), marks[1])
        pair = sum_whole(places, keep, swap(other, 0, 2), marks[2])
        line = sum_whole(places, pair, swap(pair, 0, 4), (*marks[3], *rims[4:6]))
        line = join(places, 2, line, swap(line, 0, 2), (key_grad,))
        mate = swap(line, 0, 1)
        weight_grad = jnp.where(
            core == 0, jnp.concatenate([line, mate], 1), jnp.concatenate([mate, line], 1)
        ).astype(jnp.float32)
    else:
        summed = lax.psum_scatter(
            jnp.einsum("th,td->hd", rows, grads, preferred_element_type=jnp.float32),
            ("dp", "seq"),
            scatter_dimension=0,
            tiled=True,
        )
        weight_grad = lax.all_gather(summed, "seq", axis=0, tiled=True)
    return (results[0][None], key_grad[None], value_grad[None], weight_grad)


def solution(mesh):
    token = P("dp", "seq", None)
    return jax.shard_map(
        body,
        mesh=mesh,
        in_specs=(token,) * 4
        + (P("dp", None, "seq"), token, P("dp", None), P("dp", None, None)),
        out_specs=(token, token, token, P("dp", None)),
        check_vma=False,
    )
```

```python
import functools
import math

import jax
import jax.numpy as jnp
from jax import lax
from jax.experimental import pallas as pl
from jax.experimental.pallas import tpu as pltpu
from jax.sharding import PartitionSpec as P

TILE = 384
HD = 128
VMEM = 56 * 1024 * 1024
NT = (((1,), (1,)), ((), ()))
TN = (((0,), (0,)), ((), ()))


def mm(a, b, dims=(((1,), (0,)), ((), ()))):
    return lax.dot_general(a, b, dims, preferred_element_type=jnp.float32)


def weight_kernel(places, out_ref, grad_ref, *refs):
    refs[-1][0] = mm(out_ref[...], grad_ref[...], TN).astype(jnp.bfloat16)


def weight_part(places, rows, grads, send, after=()):
    tokens, width = rows.shape
    high = width // 4
    wide = grads.shape[1] // 2

    def half(at):
        return 1 - at[1] if send else at[1]

    def out_at(p, at):
        swapped = (p % 2) * 2 + p // 2
        return (0, at[0] ^ jnp.where(half(at) == 0, swapped, p))

    return pl.pallas_call(
        weight_kernel,
        grid_spec=pltpu.PrefetchScalarGridSpec(
            num_scalar_prefetch=1,
            grid=(4,),
            in_specs=[
                pl.BlockSpec((tokens, high), out_at),
                pl.BlockSpec((tokens, wide), lambda p, at: (0, half(at))),
                *[pl.BlockSpec(memory_space=pl.ANY)] * len(after),
            ],
            out_specs=pl.BlockSpec((1, high, wide), lambda p, at: (p, 0, 0)),
        ),
        out_shape=jax.ShapeDtypeStruct((4, high, wide), jnp.bfloat16),
        compiler_params=pltpu.CompilerParams(vmem_limit_bytes=VMEM),
        cost_estimate=pl.CostEstimate(
            flops=tokens * width * grads.shape[1],
            bytes_accessed=tokens * width * 2 + tokens * grads.shape[1] + width * grads.shape[1],
            transcendentals=0,
        ),
    )(places, rows, grads, *after)


def sum_kernel(count, places, *refs):
    a0, b0, a1, b1 = refs[:4]
    keep_ref, send_ref = refs[4 + count :]
    f32 = jnp.float32
    keep_ref[...] = (a0[...].astype(f32) + b0[...].astype(f32)).astype(jnp.bfloat16)
    send_ref[...] = (a1[...].astype(f32) + b1[...].astype(f32)).astype(jnp.bfloat16)


def line_kernel(count, places, a_ref, b_ref, *refs):
    f32 = jnp.float32
    refs[count][...] = (a_ref[...].astype(f32) + b_ref[...].astype(f32)).astype(jnp.bfloat16)


def sum_whole(places, a, b, after):
    whole = pl.BlockSpec(a.shape, lambda i, at: (0, 0))
    return pl.pallas_call(
        functools.partial(line_kernel, len(after)),
        grid_spec=pltpu.PrefetchScalarGridSpec(
            num_scalar_prefetch=1,
            grid=(1,),
            in_specs=[whole, whole] + [pl.BlockSpec(memory_space=pl.ANY)] * len(after),
            out_specs=whole,
        ),
        out_shape=jax.ShapeDtypeStruct(a.shape, jnp.bfloat16),
        compiler_params=pltpu.CompilerParams(vmem_limit_bytes=VMEM),
        cost_estimate=pl.CostEstimate(
            flops=a.size, bytes_accessed=6 * a.size, transcendentals=0
        ),
    )(places, a, b, *after)


def join_kernel(bit, count, places, mine_ref, other_ref, *refs):
    rows = mine_ref.shape[0]
    at = places[bit]
    refs[count][pl.ds(pl.multiple_of(at * rows, rows), rows)] = mine_ref[...]
    refs[count][pl.ds(pl.multiple_of((1 - at) * rows, rows), rows)] = other_ref[...]


def join(places, bit, mine, other, after):
    rows, wide = mine.shape
    whole = pl.BlockSpec((rows, wide), lambda i, at: (0, 0))
    return pl.pallas_call(
        functools.partial(join_kernel, bit, len(after)),
        grid_spec=pltpu.PrefetchScalarGridSpec(
            num_scalar_prefetch=1,
            grid=(1,),
            in_specs=[whole, whole] + [pl.BlockSpec(memory_space=pl.ANY)] * len(after),
            out_specs=pl.BlockSpec((2 * rows, wide), lambda i, at: (0, 0)),
        ),
        out_shape=jax.ShapeDtypeStruct((2 * rows, wide), mine.dtype),
        compiler_params=pltpu.CompilerParams(vmem_limit_bytes=VMEM),
        cost_estimate=pl.CostEstimate(
            flops=mine.size, bytes_accessed=8 * mine.size, transcendentals=0
        ),
    )(places, mine, other, *after)


def pick_kernel(count, places, x_ref, y_ref, *refs):
    @pl.when(places[1] == 0)
    def _():
        refs[count][...] = x_ref[...]

    @pl.when(places[1] != 0)
    def _():
        refs[count][...] = y_ref[...]


def pick(places, for_first, for_second, after):
    whole = pl.BlockSpec(for_first.shape, lambda i, at: (0, 0))
    return pl.pallas_call(
        functools.partial(pick_kernel, len(after)),
        grid_spec=pltpu.PrefetchScalarGridSpec(
            num_scalar_prefetch=1,
            grid=(1,),
            in_specs=[whole, whole] + [pl.BlockSpec(memory_space=pl.ANY)] * len(after),
            out_specs=whole,
        ),
        out_shape=jax.ShapeDtypeStruct(for_first.shape, for_first.dtype),
        compiler_params=pltpu.CompilerParams(vmem_limit_bytes=VMEM),
        cost_estimate=pl.CostEstimate(
            flops=0, bytes_accessed=6 * for_first.size, transcendentals=0
        ),
    )(places, for_first, for_second, *after)


def sum_and_cut(places, bit, a, b, after=()):
    size, wide = a.shape[0] // 2, a.shape[1]
    chunk = min(size, 192)
    steps = size // chunk

    def half(at):
        return 0 if bit is None else at[bit]

    kept = pl.BlockSpec((chunk, wide), lambda i, at: (half(at) * steps + i, 0))
    sent = pl.BlockSpec((chunk, wide), lambda i, at: ((1 - half(at)) * steps + i, 0))
    out = pl.BlockSpec((chunk, wide), lambda i, at: (i, 0))
    return pl.pallas_call(
        functools.partial(sum_kernel, len(after)),
        grid_spec=pltpu.PrefetchScalarGridSpec(
            num_scalar_prefetch=1,
            grid=(steps,),
            in_specs=[kept, kept, sent, sent] + [pl.BlockSpec(memory_space=pl.ANY)] * len(after),
            out_specs=[out, out],
        ),
        out_shape=[jax.ShapeDtypeStruct((size, wide), jnp.bfloat16)] * 2,
        compiler_params=pltpu.CompilerParams(vmem_limit_bytes=VMEM),
        cost_estimate=pl.CostEstimate(
            flops=a.size, bytes_accessed=6 * a.size, transcendentals=0
        ),
    )(places, a, b, a, b, *after)


def attend_kernel(scale, halves, extra, places, *refs):
    weights = refs[: 2 if halves else 1]
    refs = refs[len(weights) :]
    (grad_ref, q_ref, o_ref, norm_ref, k_ref, v_ref, below_ref, above_ref) = refs[:8]
    refs = refs[8 + extra :]
    (dq_ref, dk_ref, dv_ref, low_ref, high_ref) = refs[:5]
    (full, attn_grad, kwin, vwin, kflip, kcat, vcat, fcat, dk, dv) = refs[5:]
    head = pl.program_id(0)
    tokens = q_ref.shape[0]
    tiles = tokens // TILE

    @pl.when(head == 0)
    def _():
        if halves:
            rows = weights[0].shape[0]
            mine = pl.multiple_of(places[1] * rows, rows)
            other = pl.multiple_of((1 - places[1]) * rows, rows)
            full[pl.ds(mine, rows)] = weights[0][...]
            full[pl.ds(other, rows)] = weights[1][...]
            block = full[...]
        else:
            block = weights[0][...]
        got = mm(grad_ref[...], block, NT).astype(jnp.bfloat16)
        for i in range(attn_grad.shape[0]):
            attn_grad[i] = got[:, i * HD : (i + 1) * HD]

    kwin[0] = below_ref[0]
    vwin[0] = below_ref[1]
    for t in range(tiles):
        kwin[t + 1] = k_ref[t * TILE : (t + 1) * TILE]
        vwin[t + 1] = v_ref[t * TILE : (t + 1) * TILE]
    kwin[tiles + 1] = above_ref[0]
    vwin[tiles + 1] = above_ref[1]
    for w in range(tiles + 2):
        kflip[w] = kwin[w].T
    dk[...] = jnp.zeros_like(dk)
    dv[...] = jnp.zeros_like(dv)
    log2e = 1.0 / math.log(2.0)

    def rows_of(t):
        return slice(t * TILE, (t + 1) * TILE)

    def products(t):
        kept = [places[4 + t * 3 + n] for n in range(3)]
        for n, w in enumerate(kept):
            part = slice(n * TILE, (n + 1) * TILE)
            kcat[t, part] = kwin[w]
            vcat[t, part] = vwin[w]
            fcat[t, :, part] = kflip[w]
        q, do = q_ref[rows_of(t)], attn_grad[head, rows_of(t)]
        return kept, mm(kcat[t], q, NT), mm(vcat[t], do, NT)

    ahead = products(0)
    for t in range(tiles):
        kept, scores, prob = ahead
        if t + 1 < tiles:
            ahead = products(t + 1)
        rows = rows_of(t)
        q, do = q_ref[rows], attn_grad[head, rows]
        norm = norm_ref[0, :, rows] * log2e
        both = do.astype(jnp.float32) * o_ref[rows].astype(jnp.float32)
        delta = both.T.sum(0, keepdims=True)
        p = jnp.exp2(scores * (scale * log2e) - norm)
        ds = (p * (prob - delta)).astype(jnp.bfloat16)
        dv_all = mm(p.astype(jnp.bfloat16), do)
        dk_all = mm(ds, q)
        dq_ref[rows] = (mm(fcat[t], ds) * scale).T.astype(jnp.bfloat16)
        for n, w in enumerate(kept):
            part = slice(n * TILE, (n + 1) * TILE)
            dv[w] += dv_all[part]
            dk[w] += dk_all[part]
    for t in range(tiles):
        dk_ref[rows_of(t)] = dk[t + 1].astype(jnp.bfloat16)
        dv_ref[rows_of(t)] = dv[t + 1].astype(jnp.bfloat16)
    low_ref[0] = dk[0].astype(jnp.bfloat16)
    low_ref[1] = dv[0].astype(jnp.bfloat16)
    high_ref[0] = dk[tiles + 1].astype(jnp.bfloat16)
    high_ref[1] = dv[tiles + 1].astype(jnp.bfloat16)


def attend(places, step, heads, weights, grads, query, attn_out, norm, keys, values, halos, before, after=()):
    tokens, width = query.shape
    tiles = tokens // TILE
    group = heads * HD
    depth = grads.shape[1]

    def at_head(h, at):
        return (0, (at[0] ^ step) * heads + h)

    def column(rows):
        return pl.BlockSpec((rows, HD), at_head)

    whole = [pl.BlockSpec(w.shape, lambda h, at: (0, 0)) for w in (*weights, grads)]
    in_specs = [
        *whole,
        column(tokens),
        column(tokens),
        pl.BlockSpec((1, 1, tokens), lambda h, at: ((at[0] ^ step) * heads + h, 0, 0)),
        column(tokens),
        column(tokens),
        *[pl.BlockSpec((2, TILE, HD), lambda h, at: (0, 0, (at[0] ^ step) * heads + h))] * 2,
    ]
    operands = [*weights, grads, query, attn_out, norm, keys, values, *halos]
    aliases = {}
    if before is not None:
        aliases = {len(operands) + 1 + i: i for i in range(3)}
        operands += before
    operands += after
    extra = len(operands) - len(in_specs)
    in_specs += [pl.BlockSpec(memory_space=pl.ANY)] * extra
    rim = pl.BlockSpec((2, TILE, HD), lambda h, at: (0, 0, h))
    kept = 3
    return pl.pallas_call(
        functools.partial(attend_kernel, 1.0 / math.sqrt(HD), len(weights) == 2, extra),
        grid_spec=pltpu.PrefetchScalarGridSpec(
            num_scalar_prefetch=1,
            grid=(heads,),
            in_specs=in_specs,
            out_specs=[column(tokens)] * 3 + [rim, rim],
            scratch_shapes=[
                pltpu.VMEM((group, depth), jnp.bfloat16),
                pltpu.VMEM((heads, tokens, HD), jnp.bfloat16),
                pltpu.VMEM((tiles + 2, TILE, HD), jnp.bfloat16),
                pltpu.VMEM((tiles + 2, TILE, HD), jnp.bfloat16),
                pltpu.VMEM((tiles + 2, HD, TILE), jnp.bfloat16),
                pltpu.VMEM((tiles, kept * TILE, HD), jnp.bfloat16),
                pltpu.VMEM((tiles, kept * TILE, HD), jnp.bfloat16),
                pltpu.VMEM((tiles, HD, kept * TILE), jnp.bfloat16),
                pltpu.VMEM((tiles + 2, TILE, HD), jnp.float32),
                pltpu.VMEM((tiles + 2, TILE, HD), jnp.float32),
            ],
        ),
        out_shape=[
            *[jax.ShapeDtypeStruct((tokens, width), jnp.bfloat16)] * 3,
            jax.ShapeDtypeStruct((2, TILE, group), jnp.bfloat16),
            jax.ShapeDtypeStruct((2, TILE, group), jnp.bfloat16),
        ],
        input_output_aliases=aliases,
        compiler_params=pltpu.CompilerParams(vmem_limit_bytes=VMEM),
        cost_estimate=pl.CostEstimate(
            flops=2 * tokens * depth * group + 20 * tokens * kept * TILE * group,
            bytes_accessed=2 * tokens * depth + 2 * depth * group + 24 * tokens * group,
            transcendentals=heads * tokens * kept * TILE,
        ),
    )(places, *operands)


def finish_kernel(scale, places, dk_ref, dv_ref, *refs):
    rims, (key_ref, value_ref) = refs[:-2], refs[-2:]
    tokens = dk_ref.shape[0]
    tiles = tokens // TILE
    f32 = jnp.float32
    for step in range(len(rims) // 2):

        @pl.when(pl.program_id(0) == step)
        def _(below=rims[2 * step], above=rims[2 * step + 1]):
            for t in range(tiles):
                rows = slice(t * TILE, (t + 1) * TILE)
                key, value = dk_ref[rows].astype(f32), dv_ref[rows].astype(f32)
                if t == 0:
                    key, value = key + below[0].astype(f32), value + below[1].astype(f32)
                if t == tiles - 1:
                    key, value = key + above[0].astype(f32), value + above[1].astype(f32)
                key_ref[rows] = (key * scale).astype(jnp.bfloat16)
                value_ref[rows] = value.astype(jnp.bfloat16)


def finish(places, dk, dv, rims):
    tokens, width = dk.shape
    steps = len(rims) // 2
    group = width // steps
    rim = pl.BlockSpec((2, TILE, group), lambda j, at: (0, 0, 0))
    placed = pl.BlockSpec((tokens, group), lambda j, at: (0, at[0] ^ j))
    return pl.pallas_call(
        functools.partial(finish_kernel, 1.0 / math.sqrt(HD)),
        grid_spec=pltpu.PrefetchScalarGridSpec(
            num_scalar_prefetch=1,
            grid=(steps,),
            in_specs=[placed, placed] + [rim] * len(rims),
            out_specs=[placed, placed],
        ),
        out_shape=[jax.ShapeDtypeStruct((tokens, width), jnp.bfloat16)] * 2,
        compiler_params=pltpu.CompilerParams(vmem_limit_bytes=VMEM),
        cost_estimate=pl.CostEstimate(
            flops=4 * tokens * width, bytes_accessed=12 * tokens * width, transcendentals=0
        ),
    )(places, dk, dv, *rims)


def body(query, key_states, value_states, attn_out, log_norm, out_grad, out_weight, tile_lists):
    dp_size, seq_size = lax.axis_size("dp"), lax.axis_size("seq")
    cube = dp_size == 4 and seq_size == 8
    query, keys, values, rows = query[0], key_states[0], value_states[0], attn_out[0]
    grads = out_grad[0]
    norm = log_norm[0][:, None, :]
    tokens, width = query.shape
    tiles = tokens // TILE
    head_count = norm.shape[0]
    steps = 4
    heads = head_count // steps
    high = width // steps
    dp, seq = lax.axis_index("dp"), lax.axis_index("seq")
    core = seq % 2
    own = lax.dynamic_slice_in_dim(tile_lists[0], seq * tiles, tiles, 0)
    kept = (own - (seq * tiles - 1)).reshape(-1).astype(jnp.int32)
    first = dp if cube else jnp.int32(0)
    bits = jnp.stack([first, core, (seq // 2) % 2, seq // 4]).astype(jnp.int32)
    places = jnp.concatenate([bits, kept])

    def send(value, partner):
        pairs = []
        for a in range(dp_size):
            for b in range(seq_size):
                to, at = partner(a, b)
                pairs.append((a * seq_size + b, to * seq_size + at))
        return lax.ppermute(value, ("dp", "seq"), pairs)

    def swap(value, dp_bit, seq_bit):
        return send(value, lambda a, b: (a ^ dp_bit, b ^ seq_bit))

    def swap_by_core(value, bits):
        return send(value, lambda a, b: (a ^ bits[b % 2], b))

    def along(value, by):
        pairs = [(i, i + by) for i in range(seq_size) if 0 <= i + by < seq_size]
        return lax.ppermute(value, "seq", pairs)

    if cube:
        half = lax.dynamic_slice_in_dim(out_weight, core * (high // 2), high // 2, 0)
        by_x, by_y = swap(half, 1, 0), swap(half, 2, 0)
        blocks = [[out_weight]] + [[b, swap(b, 0, 1)] for b in (by_x, by_y)]
    else:
        gathered = lax.all_gather(out_weight, "dp", axis=0, tiled=True)
        blocks = [[gathered[i * high : (i + 1) * high]] for i in range(steps)]

    halos = [
        along(jnp.stack([keys[tokens - TILE :], values[tokens - TILE :]]), 1),
        along(jnp.stack([keys[:TILE], values[:TILE]]), -1),
    ]

    first_after = ()
    if cube:
        wide = grads.shape[1] // 2
        sent = swap(weight_part(places, rows, grads, True), 0, 1).reshape(width, wide)
        mine = weight_part(places, rows, grads, False).reshape(width, wide)
        chip_keep, chip_send = sum_and_cut(places, None, mine, sent, (by_x, by_y, *halos))
        chip_got = swap_by_core(chip_send, (1, 2))
        first_after = (chip_send,)

    results, rims, marks = None, [], []
    for step in range(steps):
        if cube and step == 1:
            keep, other = sum_and_cut(places, None, chip_keep, chip_got, marks[0])
            by_both = swap_by_core(pick(places, by_x, by_y, (other,)), (2, 1))
        if cube and step == 2:
            blocks.append([by_both, swap(pick(places, by_both, by_both, marks[1]), 0, 1)])
        after = first_after if step == 0 else rims[2 * step - 4 : 2 * step - 2] if step > 1 else ()
        *results, low_rim, high_rim = attend(
            places, step, heads, blocks[step], grads, query, rows, norm, keys, values, halos, results, after
        )
        rims += [along(high_rim, 1), along(low_rim, -1)]
        marks.append((low_rim,))
    key_grad, value_grad = finish(places, results[1], results[2], rims)

    if cube:
        keep, other = sum_and_cut(places, 2, keep, swap_by_core(other, (2, 1)), marks[1])
        pair = sum_whole(places, keep, swap(other, 0, 2), marks[2])
        line = sum_whole(places, pair, swap(pair, 0, 4), (*marks[3], *rims[4:6]))
        line = join(places, 2, line, swap(line, 0, 2), (key_grad,))
        mate = swap(line, 0, 1)
        weight_grad = jnp.where(
            core == 0, jnp.concatenate([line, mate], 1), jnp.concatenate([mate, line], 1)
        ).astype(jnp.float32)
    else:
        summed = lax.psum_scatter(
            jnp.einsum("th,td->hd", rows, grads, preferred_element_type=jnp.float32),
            ("dp", "seq"),
            scatter_dimension=0,
            tiled=True,
        )
        weight_grad = lax.all_gather(summed, "seq", axis=0, tiled=True)
    return (results[0][None], key_grad[None], value_grad[None], weight_grad)


def solution(mesh):
    token = P("dp", "seq", None)
    return jax.shard_map(
        body,
        mesh=mesh,
        in_specs=(token,) * 4
        + (P("dp", None, "seq"), token, P("dp", None), P("dp", None, None)),
        out_specs=(token, token, token, P("dp", None)),
        check_vma=False,
    )
```
